32 devices in a mesh: grp: 2 (over core), head: 4 (over y, x), seq: 4 (over z).
Axes of the slice: x: 2, y: 2, z: 4, core: 2. Of those that a mesh axis runs over, the one named last changes fastest.
Arguments:
- seq_in: bfloat16 [4096, 4096], P('seq', 'head'), may hold values from -36 to 36
- w_proj: bfloat16 [2, 3, 4096, 4096], P('grp', None, None, 'head')
- w_out: bfloat16 [2, 4096, 4096], P('grp', 'head'), may hold values from -0.09375 to 0.09375
- filters: float32 [4096, 4096], P(('head', 'seq'))
Outputs:
- paired: bfloat16 [2, 4096, 4096], P('grp', 'seq', 'head')
- grad_filters: float32 [4096, 4096], P(('head', 'seq'), 'grp')
The draws below stay inside these ranges and needn't reach their ends.
All inputs are finite; a program needn't handle non-finite values.
Results may differ from the reference program's by a relative error of at most 0.015.
Values may be sent and summed in bfloat16 or wider, within the bound.
A program may use at most 256 MiB of HBM per device.

```python
import math
import jax
import jax.numpy as jnp
from jax import lax

D = 4096
HD = 128
L = 4096


def draw_seq_in(key, part):
    base = jax.random.normal(jax.random.fold_in(key, 11), (L, D), jnp.float32)
    base = jnp.clip(base, -6.0, 6.0)
    return base.astype(jnp.bfloat16)


def draw_w_proj(key, part):
    raw = jax.random.normal(jax.random.fold_in(key, 21), (2, 3, D, D), jnp.float32)
    raw = jnp.clip(raw, -6.0, 6.0) * D ** (-0.5)
    return raw.astype(jnp.bfloat16)


def draw_filters(key, part):
    places = jnp.arange(L, dtype=jnp.float32)
    lograte = jax.random.uniform(jax.random.fold_in(key, 31), (D,), jnp.float32, math.log(1.0 / (4 * L)), math.log(1.0 / 40))
    noise = jnp.clip(jax.random.normal(jax.random.fold_in(key, 32), (D, L), jnp.float32), -6.0, 6.0)
    rate = jnp.exp(lograte)
    energy = (1.0 - jnp.exp(-2.0 * rate * L)) / (1.0 - jnp.exp(-2.0 * rate))
    return noise * jnp.exp(-rate[:, None] * places[None, :]) * jnp.sqrt(L / energy)[:, None]


def block_scale(key, extent, cuts, low, high):
    level, own = 1.0, jax.random.fold_in(key, 6)
    for axis_at, shards_of in cuts:
        draws = jnp.exp(jax.random.uniform(jax.random.fold_in(own, axis_at), (shards_of,), jnp.float32, low / len(cuts), high / len(cuts)))
        level = level * jnp.repeat(draws, extent[axis_at] // shards_of).reshape([-1 if axis == axis_at else 1 for axis in range(len(extent))])
    return level


def bell_draw(key, shape, scale, limit, split=(), kind=jnp.bfloat16):
    drawn = jax.random.normal(key, shape, jnp.float32) * scale
    if len(split) > 0:
        drawn = block_scale(key, shape, split, -0.22, 0.18) * drawn
    return jnp.clip(drawn, min=-limit, max=limit).astype(kind)


def setup_inputs(seed: int = 0) -> dict:
    splits = jax.random.split(jax.random.key(seed), 5)
    return {
        "seq_in": draw_seq_in(jax.random.fold_in(splits[4], 71), 0),
        "w_proj": draw_w_proj(jax.random.fold_in(splits[4], 71), 0),
        "w_out": bell_draw(splits[2], (2, D, D), D ** -0.5, 0.09375, ((0, 2), (1, 4))),
        "filters": draw_filters(jax.random.fold_in(splits[4], 71), 0),
    }


def attend_heads(query, keys, values):
    length = query.shape[0]
    places = jnp.arange(length, dtype=jnp.int32)
    causal = places[None, :] <= places[:, None]
    factor = HD ** -0.5

    def one_head(triple):
        head_q, head_k, head_v = triple
        scores = jnp.dot(head_q, head_k.T, preferred_element_type=jnp.float32) * factor
        scores = jnp.where(causal, scores, -jnp.inf)
        highest = jnp.max(scores, axis=1, keepdims=True)
        expos = jnp.exp(scores - highest)
        totals = jnp.sum(expos, axis=1, keepdims=True)
        return jnp.dot(expos.astype(jnp.bfloat16), head_v, preferred_element_type=jnp.float32) / totals

    shaped = tuple(member.reshape(length, -1, HD).transpose(1, 0, 2) for member in (query, keys, values))
    heads_out = lax.map(one_head, shaped)
    return heads_out.transpose(1, 0, 2).reshape(length, -1).astype(jnp.bfloat16)


def spectra_of(signal, along):
    return jnp.fft.rfft(signal, n=2 * L, axis=along)


def back_of(spectrum):
    return jnp.fft.irfft(spectrum, n=2 * L, axis=0)[:L]


def reference(seq_in, w_proj, w_out, filters):
    def project(group):
        return [jnp.dot(seq_in, w_proj[group, which], preferred_element_type=jnp.float32).astype(jnp.bfloat16) for which in range(3)]

    query, keys_t, values_t = project(0)
    attended = attend_heads(query, keys_t, values_t)
    target = jnp.dot(attended, w_out[0], preferred_element_type=jnp.float32).astype(jnp.bfloat16)
    value_s, gate_in, gate_out = project(1)
    taps = filters * (L ** -0.5)
    carried = gate_in.astype(jnp.float32) * value_s.astype(jnp.float32)
    spec_u = spectra_of(carried, 0)
    spec_h = spectra_of(taps, 1).T
    conv = back_of(spec_u * spec_h)
    gated = (gate_out.astype(jnp.float32) * conv).astype(jnp.bfloat16)
    student = jnp.dot(gated, w_out[1], preferred_element_type=jnp.float32).astype(jnp.bfloat16)
    diff = (student.astype(jnp.float32) - target.astype(jnp.float32)).astype(jnp.bfloat16)
    d_gated = jnp.dot(diff, w_out[1].T, preferred_element_type=jnp.float32).astype(jnp.bfloat16)
    d_conv = gate_out.astype(jnp.float32) * d_gated.astype(jnp.float32)
    d_gate_out = (conv * d_gated.astype(jnp.float32)).astype(jnp.bfloat16)
    spec_d = spectra_of(d_conv, 0)
    d_carried = back_of(jnp.conj(spec_h) * spec_d)
    d_taps = back_of(jnp.conj(spec_u) * spec_d)
    d_gate_in = (d_carried * value_s.astype(jnp.float32)).astype(jnp.bfloat16)
    d_value = (d_carried * gate_in.astype(jnp.float32)).astype(jnp.bfloat16)
    grad_in = jnp.dot(d_value, w_proj[1, 0].T, preferred_element_type=jnp.float32)
    grad_in = grad_in + jnp.dot(d_gate_in, w_proj[1, 1].T, preferred_element_type=jnp.float32)
    grad_in = grad_in + jnp.dot(d_gate_out, w_proj[1, 2].T, preferred_element_type=jnp.float32)
    paired = jnp.stack([target, grad_in.astype(jnp.bfloat16)])
    grad_filters = (d_taps * (L ** -0.5)).T
    return (paired, grad_filters)
```

```python
import functools
import math

import jax
import jax.numpy as jnp
import numpy as np
from jax import lax
from jax.experimental import pallas as pl
from jax.experimental.pallas import tpu as pltpu
from jax.sharding import PartitionSpec as P

HD = 128
GROUP = 16
very_low = -1e30


def passed_along(value, axis, by):
    devices = lax.axis_size(axis)
    pairs = [(i, i + by) for i in range(devices) if 0 <= i + by < devices]
    return lax.ppermute(value, axis, pairs)


def dft_tables(length):
    total_len = 2 * length
    outer_len = total_len // 128
    half_len = outer_len // 2
    outer_idx = np.arange(outer_len)
    inner_idx = np.arange(128)
    outer = -2.0 * np.pi / outer_len * (outer_idx[:, None] * outer_idx[None, :] % outer_len)
    inner = -2.0 * np.pi / 128 * (inner_idx[:, None] * inner_idx[None, :] % 128)
    twist = -2.0 * np.pi / total_len * (outer_idx[:, None] * inner_idx[None, :] % total_len)
    cos_in, sin_in = np.cos(inner), np.sin(inner)
    first = np.concatenate([np.cos(outer)[:, :half_len], np.sin(outer)[:, :half_len]], axis=0)
    last = np.concatenate([np.cos(outer)[:half_len], np.sin(outer)[:half_len]], axis=1)
    first = np.kron(np.eye(max(1, 256 // half_len)), first)
    last = np.kron(np.eye(max(1, 256 // (2 * outer_len))), last)
    forward = np.block([[cos_in, sin_in], [-sin_in, cos_in]])
    inverse = np.block([[cos_in, -sin_in], [sin_in, cos_in]])
    narrow = [jnp.asarray(t, jnp.bfloat16) for t in (first, forward, inverse, last)]
    return (*narrow, jnp.asarray(np.cos(twist), jnp.float32), jnp.asarray(np.sin(twist), jnp.float32))


def product(a, b):
    return jnp.dot(a, b, preferred_element_type=jnp.float32)


def paired_rows(table, rows):
    depth = table.shape[1]
    out = []
    for at in range(0, rows.shape[0], 2 * depth):
        both = jnp.concatenate([rows[at : at + depth], rows[at + depth : at + 2 * depth]], axis=1)
        mixed = product(table, both)
        out += [mixed[:, :128], mixed[:, 128:]]
    return jnp.concatenate(out, axis=0)


def forward_dft(field, first, forward, cos_twist, sin_twist):
    channels, half_len, _ = field.shape
    outer_len = 2 * half_len
    rows = field.astype(jnp.bfloat16).reshape(channels * half_len, 128)
    mixed = paired_rows(first, rows).reshape(channels, 2 * outer_len, 128)
    real_a, imag_a = mixed[:, :outer_len], mixed[:, outer_len:]
    real_b = real_a * cos_twist - imag_a * sin_twist
    imag_b = real_a * sin_twist + imag_a * cos_twist
    both = jnp.concatenate([real_b, imag_b], axis=2).astype(jnp.bfloat16)
    spectrum = product(both.reshape(channels * outer_len, 256), forward)
    return spectrum[:, :128], spectrum[:, 128:]


def inverse_dft(real_x, imag_x, inverse, last, cos_twist, sin_twist):
    outer_len = cos_twist.shape[0]
    both = jnp.concatenate([real_x, imag_x], axis=1).astype(jnp.bfloat16)
    mixed = product(both, inverse)
    real_b = mixed[:, :128].reshape(-1, outer_len, 128)
    imag_b = mixed[:, 128:].reshape(-1, outer_len, 128)
    real_c = real_b * cos_twist + imag_b * sin_twist
    imag_c = imag_b * cos_twist - real_b * sin_twist
    rows = jnp.concatenate([real_c, imag_c], axis=1).astype(jnp.bfloat16)
    field = paired_rows(last, rows.reshape(-1, 128))
    return field.reshape(-1, outer_len // 2, 128)


def forward_kernel(
    scale, fields, filters, first, forward, inverse, last, cos_t, sin_t, gated, conv, spec_u, spec_h
):
    cos_twist, sin_twist = cos_t[...], sin_t[...]
    value_s = fields[0].astype(jnp.float32)
    gate_in = fields[1].astype(jnp.float32)
    gate_out = fields[2].astype(jnp.float32)
    real_u, imag_u = forward_dft(gate_in * value_s, first[...], forward[...], cos_twist, sin_twist)
    real_h, imag_h = forward_dft(filters[...], first[...], forward[...], cos_twist, sin_twist)
    spec_u[:, :128] = real_u.astype(spec_u.dtype)
    spec_u[:, 128:] = imag_u.astype(spec_u.dtype)
    spec_h[:, :128] = real_h.astype(spec_h.dtype)
    spec_h[:, 128:] = imag_h.astype(spec_h.dtype)
    out = scale * inverse_dft(
        real_u * real_h - imag_u * imag_h,
        real_u * imag_h + imag_u * real_h,
        inverse[...],
        last[...],
        cos_twist,
        sin_twist,
    )
    conv[...] = out
    gated[...] = (gate_out * out).astype(gated.dtype)


def backward_kernel(
    scale, fields, d_gated, conv, spec_u, spec_h, first, forward, inverse, last, cos_t, sin_t,
    d_fields, d_taps,
):
    cos_twist, sin_twist = cos_t[...], sin_t[...]
    grad = d_gated[...].astype(jnp.float32)
    d_fields[2] = (conv[...] * grad).astype(d_fields.dtype)
    d_conv = fields[2].astype(jnp.float32) * grad
    real_d, imag_d = forward_dft(d_conv, first[...], forward[...], cos_twist, sin_twist)

    def correlated(spec):
        real_s = spec[:, :128].astype(jnp.float32)
        imag_s = spec[:, 128:].astype(jnp.float32)
        return scale * inverse_dft(
            real_s * real_d + imag_s * imag_d,
            real_s * imag_d - imag_s * real_d,
            inverse[...],
            last[...],
            cos_twist,
            sin_twist,
        )

    d_carried = correlated(spec_h)
    d_fields[0] = (d_carried * fields[1].astype(jnp.float32)).astype(d_fields.dtype)
    d_fields[1] = (d_carried * fields[0].astype(jnp.float32)).astype(d_fields.dtype)
    d_taps[...] = correlated(spec_u)


def whole_spec(table):
    return pl.BlockSpec(table.shape, lambda i: (0, 0))


def student_specs(half_len):
    outer_len = 2 * half_len
    fields = pl.BlockSpec((3, GROUP, half_len, 128), lambda i: (0, i, 0, 0))
    single = pl.BlockSpec((GROUP, half_len, 128), lambda i: (i, 0, 0))
    spectrum = pl.BlockSpec((GROUP * outer_len, 256), lambda i: (i, 0))
    return fields, single, spectrum


def student_cost(channels, transforms):
    return pl.CostEstimate(
        flops=channels * transforms * 12_000_000,
        bytes_accessed=channels * transforms * 40_000,
        transcendentals=0,
    )


def student_forward(operands, tables, tap_scale):
    fields, filters = operands
    channels, length = filters.shape
    half_len = length // 128
    in_fields, single, spectrum = student_specs(half_len)
    scale = tap_scale / (2 * length)
    shape = (channels, half_len, 128)
    spec_shape = jax.ShapeDtypeStruct((channels * 2 * half_len, 256), jnp.bfloat16)
    gated, conv, spec_u, spec_h = pl.pallas_call(
        functools.partial(forward_kernel, scale),
        grid=(channels // GROUP,),
        in_specs=[in_fields, single, *map(whole_spec, tables)],
        out_specs=[single, single, spectrum, spectrum],
        out_shape=[
            jax.ShapeDtypeStruct(shape, jnp.bfloat16),
            jax.ShapeDtypeStruct(shape, jnp.float32),
            spec_shape,
            spec_shape,
        ],
        cost_estimate=student_cost(channels, 3),
        compiler_params=pltpu.CompilerParams(vmem_limit_bytes=48 * 2**20),
        name="student_forward",
    )(fields.reshape(3, *shape), filters.reshape(shape), *tables)
    return gated.reshape(channels, length), conv, spec_u, spec_h


def student_backward(operands, tables, tap_scale):
    fields, d_gated, conv, spec_u, spec_h = operands
    channels, length = d_gated.shape
    half_len = length // 128
    in_fields, single, spectrum = student_specs(half_len)
    scale = tap_scale / (2 * length)
    shape = (channels, half_len, 128)
    d_fields, d_taps = pl.pallas_call(
        functools.partial(backward_kernel, scale),
        grid=(channels // GROUP,),
        in_specs=[in_fields, single, single, spectrum, spectrum, *map(whole_spec, tables)],
        out_specs=[in_fields, single],
        out_shape=[
            jax.ShapeDtypeStruct((3, *shape), jnp.bfloat16),
            jax.ShapeDtypeStruct(shape, jnp.float32),
        ],
        cost_estimate=student_cost(channels, 3),
        compiler_params=pltpu.CompilerParams(vmem_limit_bytes=48 * 2**20),
        name="student_backward",
    )(fields.reshape(3, *shape), d_gated.reshape(shape), conv, spec_u, spec_h, *tables)
    return d_fields.reshape(3, channels, length), d_taps.reshape(channels, length)


def attend_kernel(block, factor, query, keys, values, out):
    at = pl.program_id(1)
    query_blk = query[0]

    def one_block(j, state, diagonal):
        highest, total, acc = state
        first = pl.multiple_of(j * block, block)
        scores = product(keys[0, pl.ds(first, block), :], query_blk)
        if diagonal:
            key_pos = lax.broadcasted_iota(jnp.int32, scores.shape, 0)
            query_pos = lax.broadcasted_iota(jnp.int32, scores.shape, 1)
            scores = jnp.where(key_pos <= query_pos, scores, -jnp.inf)
        new_max = jnp.maximum(highest, jnp.max(scores, axis=0, keepdims=True))
        expos = jnp.exp2((scores - new_max) * factor)
        fading = jnp.exp2((highest - new_max) * factor)
        total = total * fading + jnp.sum(expos, axis=0, keepdims=True)
        part = product(values[0, :, pl.ds(first, block)], expos.astype(jnp.bfloat16))
        return new_max, total, acc * fading + part

    state = (
        jnp.full((1, block), very_low, jnp.float32),
        jnp.zeros((1, block), jnp.float32),
        jnp.zeros((HD, block), jnp.float32),
    )
    state = lax.fori_loop(0, at, lambda j, inner: one_block(j, inner, False), state)
    _, total, acc = one_block(at, state, True)
    out[0] = (acc / total).astype(out.dtype)


def teacher_attend(fields):
    channels, length = fields.shape[1:]
    heads = channels // HD
    query, keys_t, values = fields.reshape(3, heads, HD, length)
    block = math.gcd(length, 512)
    pairs = heads * length * (length + block) // 2
    attended = pl.pallas_call(
        functools.partial(attend_kernel, block, HD ** (-0.5) * math.log2(math.e)),
        grid=(heads, length // block),
        in_specs=[
            pl.BlockSpec((1, HD, block), lambda h, i: (h, 0, i)),
            pl.BlockSpec((1, length, HD), lambda h, i: (h, 0, 0)),
            pl.BlockSpec((1, HD, length), lambda h, i: (h, 0, 0)),
        ],
        out_specs=pl.BlockSpec((1, HD, block), lambda h, i: (h, 0, i)),
        out_shape=jax.ShapeDtypeStruct((heads, HD, length), jnp.bfloat16),
        cost_estimate=pl.CostEstimate(
            flops=4 * HD * pairs, bytes_accessed=8 * channels * length, transcendentals=pairs
        ),
        compiler_params=pltpu.CompilerParams(vmem_limit_bytes=48 * 2**20),
        name="teacher_attend",
    )(query, keys_t.swapaxes(1, 2), values)
    return attended.reshape(channels, length)


def attend_gathered(projected, teacher):
    _, col_count, row_count = projected.shape
    head_count = col_count // HD
    parts = projected.reshape(3, head_count, HD, row_count)
    query = parts[0]
    first_row = lax.axis_index("seq") * row_count
    query_pos = first_row + jnp.arange(row_count, dtype=jnp.int32)
    factor = HD ** (-0.5)
    start_state = (
        jnp.full((head_count, row_count), very_low, jnp.float32),
        jnp.zeros((head_count, row_count), jnp.float32),
        jnp.zeros((head_count, HD, row_count), jnp.float32),
    )
    key_part = lax.all_gather(parts[1], "seq", axis=2, tiled=True)
    value_part = lax.all_gather(parts[2], "seq", axis=2, tiled=True)
    part_len = key_part.shape[2]
    step_len = math.gcd(part_len, 512)

    def one_block(block_no, status):
        offset = block_no * step_len
        key_blk = lax.dynamic_slice_in_dim(key_part, offset, step_len, 2)
        value_blk = lax.dynamic_slice_in_dim(value_part, offset, step_len, 2)
        key_pos = offset + jnp.arange(step_len, dtype=jnp.int32)

        def attend(inner):
            running_max, running_sum, running_acc = inner
            scores = (
                jnp.einsum("hdi,hdj->hij", query, key_blk, preferred_element_type=jnp.float32)
                * factor
            )
            scores = jnp.where(key_pos[None, None, :] <= query_pos[None, :, None], scores, -jnp.inf)
            new_max = jnp.maximum(running_max, jnp.max(scores, axis=2))
            expos = jnp.exp(scores - new_max[:, :, None])
            fading = jnp.exp(running_max - new_max)
            new_sum = running_sum * fading + jnp.sum(expos, axis=2)
            product = jnp.einsum(
                "hij,hdj->hdi",
                expos.astype(jnp.bfloat16),
                value_blk,
                preferred_element_type=jnp.float32,
            )
            return (new_max, new_sum, running_acc * fading[:, None, :] + product)

        def keep(inner):
            return inner

        return lax.cond(teacher, attend, keep, status)

    final_max, final_sum, final_acc = lax.fori_loop(0, part_len // step_len, one_block, start_state)
    attended = (
        (final_acc / jnp.where(teacher, final_sum, 1.0)[:, None, :])
        .reshape(col_count, row_count)
        .astype(jnp.bfloat16)
    )
    return attended


def body(seq_in, w_proj, w_out, filters):
    teacher = lax.axis_index("grp") == 0
    row_count = seq_in.shape[0]
    weights_in = w_proj[0]
    weights_out = w_out[0]
    col_count = weights_in.shape[2]
    seq_count = lax.axis_size("seq")
    chan_count = col_count // seq_count
    length = row_count * seq_count
    outer_len = 2 * length // 128
    tap_scale = length ** (-0.5)
    block = weights_in
    projected = lax.dot_general(
        block,
        lax.all_gather(seq_in, "head", axis=1, tiled=True),
        (((1,), (1,)), ((), ())),
        preferred_element_type=jnp.float32,
    ).astype(jnp.bfloat16)
    projected = projected.reshape(3, col_count, row_count)
    by_heads = chan_count % HD == 0
    spread = lax.all_to_all(
        projected.reshape(3, seq_count, chan_count, row_count),
        "seq",
        split_axis=1,
        concat_axis=3,
        tiled=True,
    )
    fields_c = spread.reshape(3, chan_count, length)
    tables = dft_tables(length)

    def run_student(operands):
        return student_forward(operands, tables, tap_scale)

    def run_teacher(operands):
        spec = jnp.zeros((chan_count * outer_len, 256), jnp.bfloat16)
        if by_heads:
            attended = teacher_attend(operands[0])
        else:
            attended = jnp.zeros((chan_count, length), jnp.bfloat16)
        conv = jnp.zeros((chan_count, length // 128, 128), jnp.float32)
        return attended, conv, spec, spec

    mixed, conv, spec_u, spec_h = lax.cond(teacher, run_teacher, run_student, (fields_c, filters))
    mixed = lax.all_to_all(mixed, "seq", split_axis=1, concat_axis=0, tiled=True)
    if not by_heads:
        mixed = jnp.where(teacher, attend_gathered(projected, teacher), mixed)
    y_own = lax.psum_scatter(
        lax.dot_general(
            weights_out, mixed, (((0,), (0,)), ((), ())), preferred_element_type=jnp.float32
        ).astype(jnp.bfloat16),
        "head",
        scatter_dimension=0,
        tiled=True,
    )
    target = passed_along(y_own, "grp", 1)
    diff = (y_own.astype(jnp.float32) - target.astype(jnp.float32)).astype(jnp.bfloat16)
    portion = lax.all_gather(diff, "head", axis=0, tiled=True)
    block = weights_out

    def keep_sum(current):
        return current

    def grow_sum(current):
        return jnp.dot(block, portion, preferred_element_type=jnp.float32)

    d_gated = lax.cond(
        teacher, keep_sum, grow_sum, jnp.zeros((col_count, row_count), jnp.float32)
    ).astype(jnp.bfloat16)
    d_spread = lax.all_to_all(
        d_gated.reshape(seq_count, chan_count, row_count),
        "seq",
        split_axis=0,
        concat_axis=2,
        tiled=True,
    ).reshape(chan_count, length)

    def run_backward(operands):
        return student_backward(operands, tables, tap_scale)

    def spare_backward(operands):
        return (
            jnp.zeros((3, chan_count, length), jnp.bfloat16),
            jnp.zeros((chan_count, length), jnp.float32),
        )

    d_fields, d_taps = lax.cond(
        teacher, spare_backward, run_backward, (fields_c, d_spread, conv, spec_u, spec_h)
    )
    d_rows = lax.all_to_all(d_fields, "seq", split_axis=2, concat_axis=1, tiled=True)

    def skip_grad(operand):
        return jnp.zeros((lax.axis_size("head") * col_count, row_count), jnp.float32)

    def make_grad(operand):
        return lax.dot_general(
            weights_in, operand, (((0, 2), (0, 1)), ((), ())), preferred_element_type=jnp.float32
        )

    d_input = lax.psum_scatter(
        lax.cond(teacher, skip_grad, make_grad, d_rows).astype(jnp.bfloat16),
        "head",
        scatter_dimension=0,
        tiled=True,
    )
    paired = jnp.where(teacher, y_own.T, d_input.T)[None]
    half_len = length // 2
    lower_taps = passed_along(d_taps[:, :half_len].astype(jnp.bfloat16), "grp", -1).astype(
        jnp.float32
    )
    grad_filters = jnp.where(teacher, lower_taps, d_taps[:, half_len:])
    return (paired, grad_filters)


def solution(mesh):
    return jax.shard_map(
        body,
        mesh=mesh,
        in_specs=(
            P("seq", "head"),
            P("grp", None, None, "head"),
            P("grp", "head", None),
            P(("head", "seq"), None),
        ),
        out_specs=(P("grp", "seq", "head"), P(("head", "seq"), "grp")),
        check_vma=False,
    )
```

```python
import functools
import math

import jax
import jax.numpy as jnp
import numpy as np
from jax import lax
from jax.experimental import pallas as pl
from jax.experimental.pallas import tpu as pltpu
from jax.sharding import PartitionSpec as P

HD = 128
GROUP = 16
very_low = -1e30


def passed_along(value, axis, by):
    devices = lax.axis_size(axis)
    pairs = [(i, i + by) for i in range(devices) if 0 <= i + by < devices]
    return lax.ppermute(value, axis, pairs)


def dft_tables(length):
    total_len = 2 * length
    outer_len = total_len // 128
    half_len = outer_len // 2
    outer_idx = np.arange(outer_len)
    inner_idx = np.arange(128)
    outer = -2.0 * np.pi / outer_len * (outer_idx[:, None] * outer_idx[None, :] % outer_len)
    inner = -2.0 * np.pi / 128 * (inner_idx[:, None] * inner_idx[None, :] % 128)
    twist = -2.0 * np.pi / total_len * (outer_idx[:, None] * inner_idx[None, :] % total_len)
    cos_in, sin_in = np.cos(inner), np.sin(inner)
    first = np.concatenate([np.cos(outer)[:, :half_len], np.sin(outer)[:, :half_len]], axis=0)
    last = np.concatenate([np.cos(outer)[:half_len], np.sin(outer)[:half_len]], axis=1)
    first = np.kron(np.eye(max(1, 256 // half_len)), first)
    last = np.kron(np.eye(max(1, 256 // (2 * outer_len))), last)
    forward = np.block([[cos_in, sin_in], [-sin_in, cos_in]])
    inverse = np.block([[cos_in, -sin_in], [sin_in, cos_in]])
    narrow = [jnp.asarray(t, jnp.bfloat16) for t in (first, forward, inverse, last)]
    return (*narrow, jnp.asarray(np.cos(twist), jnp.float32), jnp.asarray(np.sin(twist), jnp.float32))


def product(a, b):
    return jnp.dot(a, b, preferred_element_type=jnp.float32)


def paired_rows(table, rows):
    depth = table.shape[1]
    out = []
    for at in range(0, rows.shape[0], 2 * depth):
        both = jnp.concatenate([rows[at : at + depth], rows[at + depth : at + 2 * depth]], axis=1)
        mixed = product(table, both)
        out += [mixed[:, :128], mixed[:, 128:]]
    return jnp.concatenate(out, axis=0)


def forward_dft(field, first, forward, cos_twist, sin_twist):
    channels, half_len, _ = field.shape
    outer_len = 2 * half_len
    rows = field.astype(jnp.bfloat16).reshape(channels * half_len, 128)
    mixed = paired_rows(first, rows).reshape(channels, 2 * outer_len, 128)
    real_a, imag_a = mixed[:, :outer_len], mixed[:, outer_len:]
    real_b = real_a * cos_twist - imag_a * sin_twist
    imag_b = real_a * sin_twist + imag_a * cos_twist
    both = jnp.concatenate([real_b, imag_b], axis=2).astype(jnp.bfloat16)
    spectrum = product(both.reshape(channels * outer_len, 256), forward)
    return spectrum[:, :128], spectrum[:, 128:]


def inverse_dft(real_x, imag_x, inverse, last, cos_twist, sin_twist):
    outer_len = cos_twist.shape[0]
    both = jnp.concatenate([real_x, imag_x], axis=1).astype(jnp.bfloat16)
    mixed = product(both, inverse)
    real_b = mixed[:, :128].reshape(-1, outer_len, 128)
    imag_b = mixed[:, 128:].reshape(-1, outer_len, 128)
    real_c = real_b * cos_twist + imag_b * sin_twist
    imag_c = imag_b * cos_twist - real_b * sin_twist
    rows = jnp.concatenate([real_c, imag_c], axis=1).astype(jnp.bfloat16)
    field = paired_rows(last, rows.reshape(-1, 128))
    return field.reshape(-1, outer_len // 2, 128)


def joined(ref, *at):
    blocks = ref.shape[len(at)]
    parts = [ref[(*at, b)].astype(jnp.float32) for b in range(blocks)]
    return jnp.concatenate(parts, axis=1)


def scatter_to(ref, value, *at):
    share = ref.shape[-2]
    for b in range(ref.shape[0]):
        ref[(b, *at)] = value[:, b * share : (b + 1) * share].astype(ref.dtype)


def forward_kernel(
    scale, fields, filters, first, forward, inverse, last, cos_t, sin_t, gated, conv, spec_u, spec_h
):
    cos_twist, sin_twist = cos_t[...], sin_t[...]
    value_s, gate_in, gate_out = joined(fields, 0), joined(fields, 1), joined(fields, 2)
    real_u, imag_u = forward_dft(gate_in * value_s, first[...], forward[...], cos_twist, sin_twist)
    real_h, imag_h = forward_dft(filters[...], first[...], forward[...], cos_twist, sin_twist)
    spec_u[:, :128] = real_u.astype(spec_u.dtype)
    spec_u[:, 128:] = imag_u.astype(spec_u.dtype)
    spec_h[:, :128] = real_h.astype(spec_h.dtype)
    spec_h[:, 128:] = imag_h.astype(spec_h.dtype)
    out = scale * inverse_dft(
        real_u * real_h - imag_u * imag_h,
        real_u * imag_h + imag_u * real_h,
        inverse[...],
        last[...],
        cos_twist,
        sin_twist,
    )
    conv[...] = out
    scatter_to(gated, gate_out * out)


def backward_kernel(
    scale, fields, d_gated, conv, spec_u, spec_h, first, forward, inverse, last, cos_t, sin_t,
    d_fields, d_taps,
):
    cos_twist, sin_twist = cos_t[...], sin_t[...]
    grad = joined(d_gated)
    scatter_to(d_fields, conv[...] * grad, 2)
    d_conv = joined(fields, 2) * grad
    real_d, imag_d = forward_dft(d_conv, first[...], forward[...], cos_twist, sin_twist)

    def correlated(spec):
        real_s = spec[:, :128].astype(jnp.float32)
        imag_s = spec[:, 128:].astype(jnp.float32)
        return scale * inverse_dft(
            real_s * real_d + imag_s * imag_d,
            real_s * imag_d - imag_s * real_d,
            inverse[...],
            last[...],
            cos_twist,
            sin_twist,
        )

    d_carried = correlated(spec_h)
    scatter_to(d_fields, d_carried * joined(fields, 1), 0)
    scatter_to(d_fields, d_carried * joined(fields, 0), 1)
    d_taps[...] = correlated(spec_u)


def whole_spec(table):
    return pl.BlockSpec(table.shape, lambda i: (0, 0))


def student_specs(half_len, blocks):
    outer_len = 2 * half_len
    share = half_len // blocks
    fields = pl.BlockSpec((3, blocks, GROUP, share, 128), lambda i: (0, 0, i, 0, 0))
    d_fields = pl.BlockSpec((blocks, 3, GROUP, share, 128), lambda i: (0, 0, i, 0, 0))
    spread = pl.BlockSpec((blocks, GROUP, share, 128), lambda i: (0, i, 0, 0))
    single = pl.BlockSpec((GROUP, half_len, 128), lambda i: (i, 0, 0))
    spectrum = pl.BlockSpec((GROUP * outer_len, 256), lambda i: (i, 0))
    return fields, d_fields, spread, single, spectrum


def student_cost(channels, transforms):
    return pl.CostEstimate(
        flops=channels * transforms * 12_000_000,
        bytes_accessed=channels * transforms * 40_000,
        transcendentals=0,
    )


def student_forward(operands, tables, tap_scale):
    fields, filters = operands
    channels, length = filters.shape
    half_len = length // 128
    blocks = fields.shape[1]
    in_fields, _, spread, single, spectrum = student_specs(half_len, blocks)
    scale = tap_scale / (2 * length)
    shape = (channels, half_len, 128)
    split = (blocks, channels, half_len // blocks, 128)
    spec_shape = jax.ShapeDtypeStruct((channels * 2 * half_len, 256), jnp.bfloat16)
    gated, conv, spec_u, spec_h = pl.pallas_call(
        functools.partial(forward_kernel, scale),
        grid=(channels // GROUP,),
        in_specs=[in_fields, single, *map(whole_spec, tables)],
        out_specs=[spread, single, spectrum, spectrum],
        out_shape=[
            jax.ShapeDtypeStruct(split, jnp.bfloat16),
            jax.ShapeDtypeStruct(shape, jnp.float32),
            spec_shape,
            spec_shape,
        ],
        cost_estimate=student_cost(channels, 3),
        compiler_params=pltpu.CompilerParams(vmem_limit_bytes=48 * 2**20),
        name="student_forward",
    )(fields.reshape(3, *split), filters.reshape(shape), *tables)
    return gated.reshape(blocks, channels, -1), conv, spec_u, spec_h


def student_backward(operands, tables, tap_scale):
    fields, d_gated, conv, spec_u, spec_h = operands
    blocks, channels, rows = d_gated.shape
    length = blocks * rows
    half_len = length // 128
    in_fields, out_fields, spread, single, spectrum = student_specs(half_len, blocks)
    scale = tap_scale / (2 * length)
    shape = (channels, half_len, 128)
    split = (blocks, channels, half_len // blocks, 128)
    d_fields, d_taps = pl.pallas_call(
        functools.partial(backward_kernel, scale),
        grid=(channels // GROUP,),
        in_specs=[in_fields, spread, single, spectrum, spectrum, *map(whole_spec, tables)],
        out_specs=[out_fields, single],
        out_shape=[
            jax.ShapeDtypeStruct((blocks, 3, *split[1:]), jnp.bfloat16),
            jax.ShapeDtypeStruct(shape, jnp.float32),
        ],
        cost_estimate=student_cost(channels, 3),
        compiler_params=pltpu.CompilerParams(vmem_limit_bytes=48 * 2**20),
        name="student_backward",
    )(fields.reshape(3, *split), d_gated.reshape(split), conv, spec_u, spec_h, *tables)
    return d_fields, d_taps.reshape(channels, length)


def attend_kernel(block, per, factor, query, keys, values, out):
    at = pl.program_id(1)
    query_blk = query[0]

    def one_block(j, state, diagonal):
        highest, total, acc = state
        first = pl.multiple_of(j * block, block)
        scores = product(keys[0, pl.ds(first, block), :], query_blk)
        if diagonal:
            key_pos = lax.broadcasted_iota(jnp.int32, scores.shape, 0)
            query_pos = lax.broadcasted_iota(jnp.int32, scores.shape, 1)
            scores = jnp.where(key_pos <= query_pos, scores, -jnp.inf)
        new_max = jnp.maximum(highest, jnp.max(scores, axis=0, keepdims=True))
        expos = jnp.exp2((scores - new_max) * factor)
        fading = jnp.exp2((highest - new_max) * factor)
        total = total * fading + jnp.sum(expos, axis=0, keepdims=True)
        part = product(values[j // per, :, pl.ds(pl.multiple_of(j % per * block, block), block)], expos.astype(jnp.bfloat16))
        return new_max, total, acc * fading + part

    state = (
        jnp.full((1, block), very_low, jnp.float32),
        jnp.zeros((1, block), jnp.float32),
        jnp.zeros((HD, block), jnp.float32),
    )
    state = lax.fori_loop(0, at, lambda j, inner: one_block(j, inner, False), state)
    _, total, acc = one_block(at, state, True)
    out[0] = (acc / total).astype(out.dtype)


def teacher_attend(fields):
    blocks, channels, rows = fields[0].shape
    heads = channels // HD
    length = blocks * rows
    query, keys_t, values = fields
    keys = keys_t.transpose(0, 2, 1).reshape(length, channels)
    keys = keys.reshape(length, heads, HD).swapaxes(0, 1)
    block = math.gcd(rows, 512)
    per = rows // block
    pairs = heads * length * (length + block) // 2
    tile = pl.BlockSpec((1, HD, block), lambda h, i: (i // per, h, i % per))
    return pl.pallas_call(
        functools.partial(attend_kernel, block, per, HD ** (-0.5) * math.log2(math.e)),
        grid=(heads, length // block),
        in_specs=[
            tile,
            pl.BlockSpec((1, length, HD), lambda h, i: (h, 0, 0)),
            pl.BlockSpec((blocks, HD, rows), lambda h, i: (0, h, 0)),
        ],
        out_specs=tile,
        out_shape=jax.ShapeDtypeStruct((blocks, channels, rows), jnp.bfloat16),
        cost_estimate=pl.CostEstimate(
            flops=4 * HD * pairs, bytes_accessed=8 * channels * length, transcendentals=pairs
        ),
        compiler_params=pltpu.CompilerParams(vmem_limit_bytes=48 * 2**20),
        name="teacher_attend",
    )(query, keys, values)


def attend_gathered(projected, teacher):
    _, col_count, row_count = projected.shape
    head_count = col_count // HD
    parts = projected.reshape(3, head_count, HD, row_count)
    query = parts[0]
    first_row = lax.axis_index("seq") * row_count
    query_pos = first_row + jnp.arange(row_count, dtype=jnp.int32)
    factor = HD ** (-0.5)
    start_state = (
        jnp.full((head_count, row_count), very_low, jnp.float32),
        jnp.zeros((head_count, row_count), jnp.float32),
        jnp.zeros((head_count, HD, row_count), jnp.float32),
    )
    key_part = lax.all_gather(parts[1], "seq", axis=2, tiled=True)
    value_part = lax.all_gather(parts[2], "seq", axis=2, tiled=True)
    part_len = key_part.shape[2]
    step_len = math.gcd(part_len, 512)

    def one_block(block_no, status):
        offset = block_no * step_len
        key_blk = lax.dynamic_slice_in_dim(key_part, offset, step_len, 2)
        value_blk = lax.dynamic_slice_in_dim(value_part, offset, step_len, 2)
        key_pos = offset + jnp.arange(step_len, dtype=jnp.int32)

        def attend(inner):
            running_max, running_sum, running_acc = inner
            scores = (
                jnp.einsum("hdi,hdj->hij", query, key_blk, preferred_element_type=jnp.float32)
                * factor
            )
            scores = jnp.where(key_pos[None, None, :] <= query_pos[None, :, None], scores, -jnp.inf)
            new_max = jnp.maximum(running_max, jnp.max(scores, axis=2))
            expos = jnp.exp(scores - new_max[:, :, None])
            fading = jnp.exp(running_max - new_max)
            new_sum = running_sum * fading + jnp.sum(expos, axis=2)
            product = jnp.einsum(
                "hij,hdj->hdi",
                expos.astype(jnp.bfloat16),
                value_blk,
                preferred_element_type=jnp.float32,
            )
            return (new_max, new_sum, running_acc * fading[:, None, :] + product)

        def keep(inner):
            return inner

        return lax.cond(teacher, attend, keep, status)

    final_max, final_sum, final_acc = lax.fori_loop(0, part_len // step_len, one_block, start_state)
    attended = (
        (final_acc / jnp.where(teacher, final_sum, 1.0)[:, None, :])
        .reshape(col_count, row_count)
        .astype(jnp.bfloat16)
    )
    return attended


def swapped(value):
    return lax.ppermute(value, "grp", [(0, 1), (1, 0)])


def to_blocks(value):
    return lax.all_to_all(value, "seq", split_axis=0, concat_axis=0, tiled=True)


def body(seq_in, w_proj, w_out, filters):
    teacher = lax.axis_index("grp") == 0
    row_count = seq_in.shape[0]
    half_rows = row_count // 2
    weights_in = w_proj[0]
    weights_out = w_out[0]
    feature_count, col_count = weights_in.shape[1:]
    seq_count = lax.axis_size("seq")
    chan_count = col_count // seq_count
    length = row_count * seq_count
    outer_len = 2 * length // 128
    tap_scale = length ** (-0.5)

    own_rows = jnp.where(teacher, seq_in[:half_rows], seq_in[half_rows:])
    own_rows = lax.all_gather(own_rows, "head", axis=1, tiled=True)
    other_rows = swapped(own_rows)
    features = jnp.concatenate(
        [jnp.where(teacher, own_rows, other_rows), jnp.where(teacher, other_rows, own_rows)], axis=0
    )
    projected, fields = [], []
    for which in range(3):
        part = lax.dot_general(
            weights_in[which],
            features,
            (((0,), (1,)), ((), ())),
            preferred_element_type=jnp.float32,
        ).astype(jnp.bfloat16)
        projected.append(part)
        fields.append(to_blocks(part.reshape(seq_count, chan_count, row_count)))
    by_heads = chan_count % HD == 0
    tables = dft_tables(length)

    def run_student(operands):
        fields, filters = operands
        return student_forward((jnp.stack(fields), filters), tables, tap_scale)

    def run_teacher(operands):
        spec = jnp.zeros((chan_count * outer_len, 256), jnp.bfloat16)
        if by_heads:
            attended = teacher_attend(operands[0])
        else:
            attended = jnp.zeros((seq_count, chan_count, row_count), jnp.bfloat16)
        conv = jnp.zeros((chan_count, length // 128, 128), jnp.float32)
        return attended, conv, spec, spec

    mixed, conv, spec_u, spec_h = lax.cond(teacher, run_teacher, run_student, (fields, filters))
    mixed = to_blocks(mixed).reshape(col_count, row_count)
    if not by_heads:
        mixed = jnp.where(teacher, attend_gathered(jnp.stack(projected), teacher), mixed)
    y_own = lax.psum_scatter(
        lax.dot_general(
            weights_out, mixed, (((0,), (0,)), ((), ())), preferred_element_type=jnp.float32
        ).astype(jnp.bfloat16),
        "head",
        scatter_dimension=0,
        tiled=True,
    )
    y_first, y_last = y_own[:, :half_rows], y_own[:, half_rows:]
    y_other = swapped(jnp.where(teacher, y_last, y_first)).astype(jnp.float32)
    y_kept = jnp.where(teacher, y_first, y_last).astype(jnp.float32)
    diff = jnp.where(teacher, y_other - y_kept, y_kept - y_other).astype(jnp.bfloat16)
    portion_last = lax.all_gather(diff, "head", axis=0, tiled=True)
    portion_first = passed_along(portion_last, "grp", 1)

    def grown(portion):
        return lax.cond(
            teacher,
            lambda current: jnp.zeros((col_count, half_rows), jnp.bfloat16),
            lambda current: jnp.dot(
                weights_out, current, preferred_element_type=jnp.float32
            ).astype(jnp.bfloat16),
            portion,
        )

    d_last = grown(portion_last)
    d_gated = jnp.concatenate([grown(portion_first), d_last], axis=1)
    d_spread = to_blocks(d_gated.reshape(seq_count, chan_count, row_count))

    def run_backward(operands):
        fields, *rest = operands
        return student_backward((jnp.stack(fields), *rest), tables, tap_scale)

    def spare_backward(operands):
        return (
            jnp.zeros((seq_count, 3, chan_count, row_count // 128, 128), jnp.bfloat16),
            jnp.zeros((chan_count, length), jnp.float32),
        )

    d_fields, d_taps = lax.cond(
        teacher, spare_backward, run_backward, (fields, d_spread, conv, spec_u, spec_h)
    )
    d_rows = to_blocks(d_fields)

    def make_grad(operand):
        rows = operand.reshape(seq_count, 3, chan_count, half_rows).swapaxes(0, 1)
        return lax.dot_general(
            weights_in,
            rows.reshape(3, col_count, half_rows),
            (((0, 2), (0, 1)), ((), ())),
            preferred_element_type=jnp.float32,
        ).astype(jnp.bfloat16)

    def skip_grad(operand):
        return jnp.zeros((feature_count, half_rows), jnp.bfloat16)

    share = half_rows // 128
    grad_first = lax.cond(teacher, skip_grad, make_grad, d_rows[:, :, :, :share])
    from_student = passed_along(grad_first, "grp", -1)
    grad_last = lax.cond(teacher, skip_grad, make_grad, d_rows[:, :, :, share:])
    d_input = lax.psum_scatter(
        jnp.where(teacher, from_student, grad_last), "head", scatter_dimension=0, tiled=True
    )
    d_first = passed_along(d_input, "grp", 1)
    paired = jnp.where(teacher, y_own, jnp.concatenate([d_first, d_input], axis=1)).T[None]
    half_len = length // 2
    lower_taps = passed_along(d_taps[:, :half_len].astype(jnp.bfloat16), "grp", -1).astype(
        jnp.float32
    )
    grad_filters = jnp.where(teacher, lower_taps, d_taps[:, half_len:])
    return (paired, grad_filters)


def solution(mesh):
    return jax.shard_map(
        body,
        mesh=mesh,
        in_specs=(
            P("seq", "head"),
            P("grp", None, None, "head"),
            P("grp", "head", None),
            P(("head", "seq"), None),
        ),
        out_specs=(P("grp", "seq", "head"), P(("head", "seq"), "grp")),
        check_vma=False,
    )
```

```python
import functools
import math

import jax
import jax.numpy as jnp
import numpy as np
from jax import lax
from jax.experimental import pallas as pl
from jax.experimental.pallas import tpu as pltpu
from jax.sharding import PartitionSpec as P

HD = 128
GROUP = 16
very_low = -1e30


def passed_along(value, axis, by):
    devices = lax.axis_size(axis)
    pairs = [(i, i + by) for i in range(devices) if 0 <= i + by < devices]
    return lax.ppermute(value, axis, pairs)


def dft_tables(length):
    total_len = 2 * length
    outer_len = total_len // 128
    half_len = outer_len // 2
    outer_idx = np.arange(outer_len)
    inner_idx = np.arange(128)
    outer = -2.0 * np.pi / outer_len * (outer_idx[:, None] * outer_idx[None, :] % outer_len)
    inner = -2.0 * np.pi / 128 * (inner_idx[:, None] * inner_idx[None, :] % 128)
    twist = -2.0 * np.pi / total_len * (outer_idx[:, None] * inner_idx[None, :] % total_len)
    cos_in, sin_in = np.cos(inner), np.sin(inner)
    first = np.concatenate([np.cos(outer)[:, :half_len], np.sin(outer)[:, :half_len]], axis=0)
    last = np.concatenate([np.cos(outer)[:half_len], np.sin(outer)[:half_len]], axis=1)
    first = np.kron(np.eye(max(1, 256 // half_len)), first)
    last = np.kron(np.eye(max(1, 256 // (2 * outer_len))), last)
    forward = np.block([[cos_in, sin_in], [-sin_in, cos_in]])
    inverse = np.block([[cos_in, -sin_in], [sin_in, cos_in]])
    narrow = [jnp.asarray(t, jnp.bfloat16) for t in (first, forward, inverse, last)]
    return (*narrow, jnp.asarray(np.cos(twist), jnp.float32), jnp.asarray(np.sin(twist), jnp.float32))


def product(a, b):
    return jnp.dot(a, b, preferred_element_type=jnp.float32)


def paired_rows(table, rows):
    depth = table.shape[1]
    out = []
    for at in range(0, rows.shape[0], 2 * depth):
        both = jnp.concatenate([rows[at : at + depth], rows[at + depth : at + 2 * depth]], axis=1)
        mixed = product(table, both)
        out += [mixed[:, :128], mixed[:, 128:]]
    return jnp.concatenate(out, axis=0)


def forward_dft(field, first, forward, cos_twist, sin_twist):
    channels, half_len, _ = field.shape
    outer_len = 2 * half_len
    rows = field.astype(jnp.bfloat16).reshape(channels * half_len, 128)
    mixed = paired_rows(first, rows).reshape(channels, 2 * outer_len, 128)
    real_a, imag_a = mixed[:, :outer_len], mixed[:, outer_len:]
    real_b = real_a * cos_twist - imag_a * sin_twist
    imag_b = real_a * sin_twist + imag_a * cos_twist
    both = jnp.concatenate([real_b, imag_b], axis=2).astype(jnp.bfloat16)
    spectrum = product(both.reshape(channels * outer_len, 256), forward)
    return spectrum[:, :128], spectrum[:, 128:]


def inverse_dft(real_x, imag_x, inverse, last, cos_twist, sin_twist):
    outer_len = cos_twist.shape[0]
    both = jnp.concatenate([real_x, imag_x], axis=1).astype(jnp.bfloat16)
    mixed = product(both, inverse)
    real_b = mixed[:, :128].reshape(-1, outer_len, 128)
    imag_b = mixed[:, 128:].reshape(-1, outer_len, 128)
    real_c = real_b * cos_twist + imag_b * sin_twist
    imag_c = imag_b * cos_twist - real_b * sin_twist
    rows = jnp.concatenate([real_c, imag_c], axis=1).astype(jnp.bfloat16)
    field = paired_rows(last, rows.reshape(-1, 128))
    return field.reshape(-1, outer_len // 2, 128)


def joined(ref, *at):
    blocks = ref.shape[len(at)]
    parts = [ref[(*at, b)].astype(jnp.float32) for b in range(blocks)]
    return jnp.concatenate(parts, axis=1)


def scatter_to(ref, value, *at):
    share = ref.shape[-2]
    for b in range(ref.shape[0]):
        ref[(b, *at)] = value[:, b * share : (b + 1) * share].astype(ref.dtype)


def forward_kernel(
    scale, fields, filters, first, forward, inverse, last, cos_t, sin_t, gated, conv, spec_u, spec_h
):
    cos_twist, sin_twist = cos_t[...], sin_t[...]
    value_s, gate_in, gate_out = joined(fields, 0), joined(fields, 1), joined(fields, 2)
    real_u, imag_u = forward_dft(gate_in * value_s, first[...], forward[...], cos_twist, sin_twist)
    real_h, imag_h = forward_dft(filters[...], first[...], forward[...], cos_twist, sin_twist)
    spec_u[:, :128] = real_u.astype(spec_u.dtype)
    spec_u[:, 128:] = imag_u.astype(spec_u.dtype)
    spec_h[:, :128] = real_h.astype(spec_h.dtype)
    spec_h[:, 128:] = imag_h.astype(spec_h.dtype)
    out = scale * inverse_dft(
        real_u * real_h - imag_u * imag_h,
        real_u * imag_h + imag_u * real_h,
        inverse[...],
        last[...],
        cos_twist,
        sin_twist,
    )
    conv[...] = out
    scatter_to(gated, gate_out * out)


def backward_kernel(
    scale, fields, d_gated, conv, spec_u, spec_h, first, forward, inverse, last, cos_t, sin_t,
    d_fields, d_taps,
):
    cos_twist, sin_twist = cos_t[...], sin_t[...]
    grad = joined(d_gated)
    scatter_to(d_fields, conv[...] * grad, 2)
    d_conv = joined(fields, 2) * grad
    real_d, imag_d = forward_dft(d_conv, first[...], forward[...], cos_twist, sin_twist)

    def correlated(spec):
        real_s = spec[:, :128].astype(jnp.float32)
        imag_s = spec[:, 128:].astype(jnp.float32)
        return scale * inverse_dft(
            real_s * real_d + imag_s * imag_d,
            real_s * imag_d - imag_s * real_d,
            inverse[...],
            last[...],
            cos_twist,
            sin_twist,
        )

    d_carried = correlated(spec_h)
    scatter_to(d_fields, d_carried * joined(fields, 1), 0)
    scatter_to(d_fields, d_carried * joined(fields, 0), 1)
    d_taps[...] = correlated(spec_u)


def whole_spec(table):
    return pl.BlockSpec(table.shape, lambda i: (0, 0))


def student_specs(half_len, blocks):
    outer_len = 2 * half_len
    share = half_len // blocks
    fields = pl.BlockSpec((3, blocks, GROUP, share, 128), lambda i: (0, 0, i, 0, 0))
    d_fields = pl.BlockSpec((blocks, 3, GROUP, share, 128), lambda i: (0, 0, i, 0, 0))
    spread = pl.BlockSpec((blocks, GROUP, share, 128), lambda i: (0, i, 0, 0))
    single = pl.BlockSpec((GROUP, half_len, 128), lambda i: (i, 0, 0))
    spectrum = pl.BlockSpec((GROUP * outer_len, 256), lambda i: (i, 0))
    return fields, d_fields, spread, single, spectrum


def student_cost(channels, transforms):
    return pl.CostEstimate(
        flops=channels * transforms * 12_000_000,
        bytes_accessed=channels * transforms * 40_000,
        transcendentals=0,
    )


def student_forward(operands, tables, tap_scale):
    fields, filters = operands
    channels, length = filters.shape
    half_len = length // 128
    blocks = fields.shape[1]
    in_fields, _, spread, single, spectrum = student_specs(half_len, blocks)
    scale = tap_scale / (2 * length)
    shape = (channels, half_len, 128)
    split = (blocks, channels, half_len // blocks, 128)
    spec_shape = jax.ShapeDtypeStruct((channels * 2 * half_len, 256), jnp.bfloat16)
    gated, conv, spec_u, spec_h = pl.pallas_call(
        functools.partial(forward_kernel, scale),
        grid=(channels // GROUP,),
        in_specs=[in_fields, single, *map(whole_spec, tables)],
        out_specs=[spread, single, spectrum, spectrum],
        out_shape=[
            jax.ShapeDtypeStruct(split, jnp.bfloat16),
            jax.ShapeDtypeStruct(shape, jnp.float32),
            spec_shape,
            spec_shape,
        ],
        cost_estimate=student_cost(channels, 3),
        compiler_params=pltpu.CompilerParams(vmem_limit_bytes=48 * 2**20),
        name="student_forward",
    )(fields.reshape(3, *split), filters.reshape(shape), *tables)
    return gated.reshape(blocks, channels, -1), conv, spec_u, spec_h


def student_backward(operands, tables, tap_scale):
    fields, d_gated, conv, spec_u, spec_h = operands
    blocks, channels, rows = d_gated.shape
    length = blocks * rows
    half_len = length // 128
    in_fields, out_fields, spread, single, spectrum = student_specs(half_len, blocks)
    scale = tap_scale / (2 * length)
    shape = (channels, half_len, 128)
    split = (blocks, channels, half_len // blocks, 128)
    d_fields, d_taps = pl.pallas_call(
        functools.partial(backward_kernel, scale),
        grid=(channels // GROUP,),
        in_specs=[in_fields, spread, single, spectrum, spectrum, *map(whole_spec, tables)],
        out_specs=[out_fields, single],
        out_shape=[
            jax.ShapeDtypeStruct((blocks, 3, *split[1:]), jnp.bfloat16),
            jax.ShapeDtypeStruct(shape, jnp.float32),
        ],
        cost_estimate=student_cost(channels, 3),
        compiler_params=pltpu.CompilerParams(vmem_limit_bytes=48 * 2**20),
        name="student_backward",
    )(fields.reshape(3, *split), d_gated.reshape(split), conv, spec_u, spec_h, *tables)
    return d_fields, d_taps.reshape(channels, length)


def attend_kernel(block, per, factor, query, keys, values, out):
    at = pl.program_id(1)
    query_blk = query[0]

    def one_block(j, state, diagonal):
        highest, total, acc = state
        first = pl.multiple_of(j * block, block)
        scores = product(keys[0, pl.ds(first, block), :], query_blk)
        if diagonal:
            key_pos = lax.broadcasted_iota(jnp.int32, scores.shape, 0)
            query_pos = lax.broadcasted_iota(jnp.int32, scores.shape, 1)
            scores = jnp.where(key_pos <= query_pos, scores, -jnp.inf)
        new_max = jnp.maximum(highest, jnp.max(scores, axis=0, keepdims=True))
        expos = jnp.exp2((scores - new_max) * factor)
        fading = jnp.exp2((highest - new_max) * factor)
        total = total * fading + jnp.sum(expos, axis=0, keepdims=True)
        part = product(values[j // per, :, pl.ds(pl.multiple_of(j % per * block, block), block)], expos.astype(jnp.bfloat16))
        return new_max, total, acc * fading + part

    state = (
        jnp.full((1, block), very_low, jnp.float32),
        jnp.zeros((1, block), jnp.float32),
        jnp.zeros((HD, block), jnp.float32),
    )
    state = lax.fori_loop(0, at, lambda j, inner: one_block(j, inner, False), state)
    _, total, acc = one_block(at, state, True)
    out[0] = (acc / total).astype(out.dtype)


def teacher_attend(fields):
    blocks, channels, rows = fields[0].shape
    heads = channels // HD
    length = blocks * rows
    query, keys_t, values = fields
    keys = keys_t.transpose(0, 2, 1).reshape(length, channels)
    keys = keys.reshape(length, heads, HD).swapaxes(0, 1)
    block = math.gcd(rows, 512)
    per = rows // block
    pairs = heads * length * (length + block) // 2
    tile = pl.BlockSpec((1, HD, block), lambda h, i: (i // per, h, i % per))
    return pl.pallas_call(
        functools.partial(attend_kernel, block, per, HD ** (-0.5) * math.log2(math.e)),
        grid=(heads, length // block),
        in_specs=[
            tile,
            pl.BlockSpec((1, length, HD), lambda h, i: (h, 0, 0)),
            pl.BlockSpec((blocks, HD, rows), lambda h, i: (0, h, 0)),
        ],
        out_specs=tile,
        out_shape=jax.ShapeDtypeStruct((blocks, channels, rows), jnp.bfloat16),
        cost_estimate=pl.CostEstimate(
            flops=4 * HD * pairs, bytes_accessed=8 * channels * length, transcendentals=pairs
        ),
        compiler_params=pltpu.CompilerParams(vmem_limit_bytes=48 * 2**20),
        name="teacher_attend",
    )(query, keys, values)


def attend_gathered(projected, teacher):
    _, col_count, row_count = projected.shape
    head_count = col_count // HD
    parts = projected.reshape(3, head_count, HD, row_count)
    query = parts[0]
    first_row = lax.axis_index("seq") * row_count
    query_pos = first_row + jnp.arange(row_count, dtype=jnp.int32)
    factor = HD ** (-0.5)
    start_state = (
        jnp.full((head_count, row_count), very_low, jnp.float32),
        jnp.zeros((head_count, row_count), jnp.float32),
        jnp.zeros((head_count, HD, row_count), jnp.float32),
    )
    key_part = lax.all_gather(parts[1], "seq", axis=2, tiled=True)
    value_part = lax.all_gather(parts[2], "seq", axis=2, tiled=True)
    part_len = key_part.shape[2]
    step_len = math.gcd(part_len, 512)

    def one_block(block_no, status):
        offset = block_no * step_len
        key_blk = lax.dynamic_slice_in_dim(key_part, offset, step_len, 2)
        value_blk = lax.dynamic_slice_in_dim(value_part, offset, step_len, 2)
        key_pos = offset + jnp.arange(step_len, dtype=jnp.int32)

        def attend(inner):
            running_max, running_sum, running_acc = inner
            scores = (
                jnp.einsum("hdi,hdj->hij", query, key_blk, preferred_element_type=jnp.float32)
                * factor
            )
            scores = jnp.where(key_pos[None, None, :] <= query_pos[None, :, None], scores, -jnp.inf)
            new_max = jnp.maximum(running_max, jnp.max(scores, axis=2))
            expos = jnp.exp(scores - new_max[:, :, None])
            fading = jnp.exp(running_max - new_max)
            new_sum = running_sum * fading + jnp.sum(expos, axis=2)
            product = jnp.einsum(
                "hij,hdj->hdi",
                expos.astype(jnp.bfloat16),
                value_blk,
                preferred_element_type=jnp.float32,
            )
            return (new_max, new_sum, running_acc * fading[:, None, :] + product)

        def keep(inner):
            return inner

        return lax.cond(teacher, attend, keep, status)

    final_max, final_sum, final_acc = lax.fori_loop(0, part_len // step_len, one_block, start_state)
    attended = (
        (final_acc / jnp.where(teacher, final_sum, 1.0)[:, None, :])
        .reshape(col_count, row_count)
        .astype(jnp.bfloat16)
    )
    return attended


def swapped(value):
    return lax.ppermute(value, "grp", [(0, 1), (1, 0)])


def to_blocks(value):
    return lax.all_to_all(value, "seq", split_axis=0, concat_axis=0, tiled=True)


def body(seq_in, w_proj, w_out, filters):
    teacher = lax.axis_index("grp") == 0
    row_count = seq_in.shape[0]
    half_rows = row_count // 2
    weights_in = w_proj[0]
    weights_out = w_out[0]
    feature_count, col_count = weights_in.shape[1:]
    seq_count = lax.axis_size("seq")
    chan_count = col_count // seq_count
    length = row_count * seq_count
    outer_len = 2 * length // 128
    tap_scale = length ** (-0.5)

    student_in = passed_along(weights_in, "grp", -1)
    student_out = passed_along(weights_out, "grp", -1)

    own_rows = jnp.where(teacher, seq_in[:half_rows], seq_in[half_rows:])
    own_rows = lax.all_gather(own_rows, "head", axis=1, tiled=True)
    other_rows = swapped(own_rows)
    features = jnp.concatenate(
        [jnp.where(teacher, own_rows, other_rows), jnp.where(teacher, other_rows, own_rows)], axis=0
    )
    projected, fields = [], []
    for which in range(3):
        part = lax.dot_general(
            weights_in[which],
            features,
            (((0,), (1,)), ((), ())),
            preferred_element_type=jnp.float32,
        ).astype(jnp.bfloat16)
        projected.append(part)
        fields.append(to_blocks(part.reshape(seq_count, chan_count, row_count)))
    by_heads = chan_count % HD == 0
    tables = dft_tables(length)

    def run_student(operands):
        fields, filters = operands
        return student_forward((jnp.stack(fields), filters), tables, tap_scale)

    def run_teacher(operands):
        spec = jnp.zeros((chan_count * outer_len, 256), jnp.bfloat16)
        if by_heads:
            attended = teacher_attend(operands[0])
        else:
            attended = jnp.zeros((seq_count, chan_count, row_count), jnp.bfloat16)
        conv = jnp.zeros((chan_count, length // 128, 128), jnp.float32)
        return attended, conv, spec, spec

    mixed, conv, spec_u, spec_h = lax.cond(teacher, run_teacher, run_student, (fields, filters))
    mixed = to_blocks(mixed).reshape(col_count, row_count)
    if not by_heads:
        mixed = jnp.where(teacher, attend_gathered(jnp.stack(projected), teacher), mixed)
    y_own = lax.psum_scatter(
        lax.dot_general(
            weights_out, mixed, (((0,), (0,)), ((), ())), preferred_element_type=jnp.float32
        ).astype(jnp.bfloat16),
        "head",
        scatter_dimension=0,
        tiled=True,
    )
    y_first, y_last = y_own[:, :half_rows], y_own[:, half_rows:]
    y_other = swapped(jnp.where(teacher, y_last, y_first)).astype(jnp.float32)
    y_kept = jnp.where(teacher, y_first, y_last).astype(jnp.float32)
    diff = jnp.where(teacher, y_other - y_kept, y_kept - y_other).astype(jnp.bfloat16)
    portion = lax.all_gather(diff, "head", axis=0, tiled=True)

    def grown(weights, current):
        return jnp.dot(weights, current, preferred_element_type=jnp.float32).astype(jnp.bfloat16)

    d_gated = lax.cond(
        teacher,
        lambda theirs, own, current: grown(theirs, current),
        lambda theirs, own, current: grown(own, current),
        student_out,
        weights_out,
        portion,
    )
    d_last = to_blocks(d_gated.reshape(seq_count, chan_count, half_rows))
    d_first = passed_along(d_last, "grp", 1)
    d_spread = jnp.concatenate([d_first, d_last], axis=2)

    share = half_rows // 128
    half_shape = (seq_count, 3, chan_count, half_rows)

    def run_backward(operands):
        fields, *rest = operands
        d_fields, d_taps = student_backward((jnp.stack(fields), *rest), tables, tap_scale)
        d_fields = d_fields.reshape(seq_count, 3, chan_count, 2 * share, 128)
        first = d_fields[:, :, :, :share].reshape(half_shape)
        return first, d_fields[:, :, :, share:].reshape(half_shape), d_taps

    def spare_backward(operands):
        spare = jnp.zeros(half_shape, jnp.bfloat16)
        return spare, spare, jnp.zeros((chan_count, length), jnp.float32)

    d_first, d_last, d_taps = lax.cond(
        teacher, spare_backward, run_backward, (fields, d_spread, conv, spec_u, spec_h)
    )
    d_rows = to_blocks(jnp.where(teacher, passed_along(d_first, "grp", -1), d_last))
    d_rows = d_rows.swapaxes(0, 1).reshape(3, col_count, half_rows)

    def make_grad(weights, rows):
        return lax.dot_general(
            weights, rows, (((0, 2), (0, 1)), ((), ())), preferred_element_type=jnp.float32
        ).astype(jnp.bfloat16)

    grad = lax.cond(
        teacher,
        lambda theirs, own, rows: make_grad(theirs, rows),
        lambda theirs, own, rows: make_grad(own, rows),
        student_in,
        weights_in,
        d_rows,
    )
    d_input = lax.psum_scatter(grad, "head", scatter_dimension=0, tiled=True)
    d_first = passed_along(d_input, "grp", 1)
    paired = jnp.where(teacher, y_own, jnp.concatenate([d_first, d_input], axis=1)).T[None]
    half_len = length // 2
    lower_taps = passed_along(d_taps[:, :half_len].astype(jnp.bfloat16), "grp", -1).astype(
        jnp.float32
    )
    grad_filters = jnp.where(teacher, lower_taps, d_taps[:, half_len:])
    return (paired, grad_filters)


def solution(mesh):
    return jax.shard_map(
        body,
        mesh=mesh,
        in_specs=(
            P("seq", "head"),
            P("grp", None, None, "head"),
            P("grp", "head", None),
            P(("head", "seq"), None),
        ),
        out_specs=(P("grp", "seq", "head"), P(("head", "seq"), "grp")),
        check_vma=False,
    )
```
